256 devices in a mesh: group: 8 (over z), ctx: 32 (over x, y, core).
Axes of the slice: x: 4, y: 4, z: 8, core: 2. Of those that a mesh axis runs over, the one named last changes fastest.
Arguments:
- queries: bfloat16 [512, 8192], P(('group', 'ctx')), may hold values from -8 to 8
- prefix_keys: bfloat16 [16, 32768, 1024], P('group', 'ctx'), may hold values from -8 to 8
- prefix_values: bfloat16 [16, 32768, 1024], P('group', 'ctx'), may hold values from -6 to 6
- suffix_keys: bfloat16 [512, 256, 1024], P(('group', 'ctx')), may hold values from -8 to 8
- suffix_values: bfloat16 [512, 256, 1024], P(('group', 'ctx')), may hold values from -6 to 6
- new_keys: bfloat16 [512, 1024], P(('group', 'ctx')), may hold values from -8 to 8
- new_values: bfloat16 [512, 1024], P(('group', 'ctx')), may hold values from -6 to 6
- suffix_lengths: int32 [512], P(('group', 'ctx')), may hold values from 1 to 256
- counts: int32 [16], P('group'), may hold values from 1 to 63, as said below
- out_weight: bfloat16 [8192, 5120], P('ctx', 'group'), may hold values from -0.0625 to 0.0625
Outputs:
- projected: bfloat16 [512, 5120], P(('group', 'ctx'))
The draws below stay inside these ranges and needn't reach their ends.
Inputs may be any that keep to these rules, and one draw needn't show every extreme that they name: `counts`: each group's 2 consecutive entries sum to 64; the samples of a group stand in the order of its prompts.
All inputs are finite; a program needn't handle non-finite values.
Results may differ from the reference program's by a relative error of at most 0.0058.
Values may be sent and summed in bfloat16 or wider, within the bound.
No kernel may reach another device: no remote copies, remote signals or barrier semaphores. Data moves between devices by JAX's collectives and lax.ppermute only.
A program may use at most 128 MiB of HBM per device.

```python
import math
import jax
import jax.numpy as jnp
from jax import lax

D = 5120
QH = 64
KVH = 8
DH = 128
POS_DEV = 1024
SAMP_DEV = 2
SUF = 256
PROMPT_GRP = 2
PREFIX = 32768
PROMPTS = 16
SAMPLES_GRP = 64
SAMPLES = 512
N_CTX = 32


def shared_parts(key):
    context = jax.random.normal(jax.random.fold_in(key, 100), (SAMPLES, KVH, DH), jnp.float32)
    return context


def draw_queries(key, part):
    context = shared_parts(key)
    key = jax.random.fold_in(key, 1)
    group_size = QH // KVH
    shape = (SAMPLES, KVH, group_size, DH)
    noise = 0.7 * jax.random.normal(key, shape, jnp.float32)
    result = 0.7 * context[:, :, None, :] + noise
    return result.reshape(SAMPLES, QH * DH).astype(jnp.bfloat16)


def draw_prefix_keys(key, part):
    key = jax.random.fold_in(key, 2)
    shape = (PROMPTS, PREFIX, KVH, DH)
    result = jax.random.normal(key, shape, jnp.float32)
    return result.reshape(PROMPTS, PREFIX, KVH * DH).astype(jnp.bfloat16)


def draw_suffix_keys(key, part):
    context = shared_parts(key)
    key = jax.random.fold_in(key, 3)
    shape = (SAMPLES, SUF, KVH, DH)
    noise = 0.7 * jax.random.normal(key, shape, jnp.float32)
    result = 0.7 * context[:, None, :, :] + noise
    return result.reshape(SAMPLES, SUF, KVH * DH).astype(jnp.bfloat16)


def draw_new_keys(key, part):
    context = shared_parts(key)
    key = jax.random.fold_in(key, 4)
    shape = (SAMPLES, KVH, DH)
    noise = 0.5 * jax.random.normal(key, shape, jnp.float32)
    result = 1.2 * context + noise
    return result.reshape(SAMPLES, KVH * DH).astype(jnp.bfloat16)


def draw_counts(key, part):
    key = jax.random.fold_in(key, 7)
    group_count = PROMPTS // PROMPT_GRP
    leading = jax.random.randint(key, (group_count,), 1, SAMPLES_GRP, dtype=jnp.int32)
    hottest = jax.random.randint(jax.random.fold_in(key, 1), (), 0, group_count, dtype=jnp.int32)
    leading = jnp.where(jnp.arange(group_count, dtype=jnp.int32) == hottest, 1, leading).astype(jnp.int32)
    return jnp.stack([leading, SAMPLES_GRP - leading], axis=1).reshape(PROMPTS).astype(jnp.int32)


def set_ends(array, rng, smallest, top_value):
    spot = [jax.random.randint(jax.random.fold_in(rng, axis), (), 0, length) for axis, length in enumerate(array.shape)]
    main_axis = array.shape.index(max(array.shape))
    next_to = spot[:main_axis] + [(spot[main_axis] + 1) % array.shape[main_axis]] + spot[main_axis + 1:]
    return array.at[tuple(spot)].set(smallest).at[tuple(next_to)].set(top_value)


def levels(own_key, extent, pieces, least, top_value):
    factor_of, own = 1.0, jax.random.fold_in(own_key, 6)
    for dim, parts in pieces:
        draws = jnp.exp(jax.random.uniform(jax.random.fold_in(own, dim), (parts,), jnp.float32, least / len(pieces), top_value / len(pieces)))
        factor_of = factor_of * jnp.repeat(draws, extent[dim] // parts).reshape([-1 if axis == dim else 1 for axis in range(len(extent))])
    return factor_of


def gaussian(stream_key, extent, deviation, limit, shards=(), kind=jnp.bfloat16):
    values = jax.random.normal(stream_key, extent, jnp.float32) * deviation
    if len(shards) > 0:
        values = levels(stream_key, extent, shards, -0.22, 0.18) * values
    return jnp.clip(values, min=-limit, max=limit).astype(kind)


def setup_inputs(seed: int = 0) -> dict:
    splits = jax.random.split(jax.random.key(seed), 11)
    queries = draw_queries(jax.random.fold_in(splits[10], 71), 0)
    prefix_keys = draw_prefix_keys(jax.random.fold_in(splits[10], 71), 0)
    prefix_values = gaussian(splits[2], (PROMPTS, PREFIX, KVH * DH), 1.0, 6.0, ((0, 8), (1, 32)))
    suffix_keys = draw_suffix_keys(jax.random.fold_in(splits[10], 71), 0)
    suffix_values = gaussian(splits[4], (SAMPLES, SUF, KVH * DH), 1.0, 6.0, ((0, 256),))
    new_keys = draw_new_keys(jax.random.fold_in(splits[10], 71), 0)
    new_values = gaussian(splits[6], (SAMPLES, KVH * DH), 1.0, 6.0, ((0, 256),))
    suffix_lengths = set_ends(jax.random.randint(splits[7], (SAMPLES,), 1, SUF + 1), jax.random.fold_in(splits[7], 1), 1, SUF).astype(jnp.int32)
    counts = draw_counts(jax.random.fold_in(splits[10], 71), 0)
    out_weight = gaussian(splits[9], (QH * DH, D), (QH * DH) ** -0.5, 0.0625, ((0, 32), (1, 8)))
    return dict(queries=queries, prefix_keys=prefix_keys, prefix_values=prefix_values, suffix_keys=suffix_keys, suffix_values=suffix_values, new_keys=new_keys, new_values=new_values, suffix_lengths=suffix_lengths, counts=counts, out_weight=out_weight)


FLOOR = -1e+30

def reference(queries, prefix_keys, prefix_values, suffix_keys, suffix_values, new_keys, new_values, suffix_lengths, counts, out_weight):
    group_size = QH // KVH
    scale_factor = 1.0 / math.sqrt(DH)
    by_group = counts.reshape(PROMPTS // PROMPT_GRP, PROMPT_GRP).astype(jnp.int32)
    bounds = jnp.cumsum(by_group, axis=1).astype(jnp.int32)
    sample_ids = jnp.arange(SAMPLES, dtype=jnp.int32)
    home_group = (sample_ids // SAMPLES_GRP).astype(jnp.int32)
    in_group = (sample_ids % SAMPLES_GRP).astype(jnp.int32)
    above = (in_group[:, None] >= bounds[home_group]).astype(jnp.int32)
    owners = (home_group * PROMPT_GRP + lax.optimization_barrier(jnp.sum(above, axis=1))).astype(jnp.int32)
    homes = (in_group // SAMP_DEV).astype(jnp.int32)

    def one_sample(item):
        query_row, owner_id, home_id, length, own_keys, own_values, self_key, self_value = item
        query_grid = query_row.astype(jnp.float32).reshape(KVH, group_size, DH)
        base_keys = lax.dynamic_index_in_dim(prefix_keys, owner_id, 0, keepdims=False).astype(jnp.float32).reshape(N_CTX, POS_DEV, KVH, DH)
        base_values = lax.dynamic_index_in_dim(prefix_values, owner_id, 0, keepdims=False).astype(jnp.float32).reshape(N_CTX, POS_DEV, KVH, DH)
        pre_scores = jnp.einsum('kgd,cpkd->kgcp', query_grid, base_keys) * scale_factor
        pre_peak = lax.optimization_barrier(jnp.max(pre_scores, axis=3))
        pre_terms = jnp.exp(pre_scores - pre_peak[..., None])
        pre_total = lax.optimization_barrier(jnp.sum(pre_terms, axis=3))
        pre_weights = lax.optimization_barrier(pre_terms.astype(jnp.bfloat16)).astype(jnp.float32)
        pre_sum = jnp.einsum('kgcp,cpkd->kgcd', pre_weights, base_values)
        suf_keys = own_keys.astype(jnp.float32).reshape(SUF, KVH, DH)
        suf_vals = own_values.astype(jnp.float32).reshape(SUF, KVH, DH)
        suf_scores = jnp.einsum('kgd,tkd->kgt', query_grid, suf_keys) * scale_factor
        position = jnp.arange(SUF, dtype=jnp.int32)
        suf_scores = jnp.where((position < length)[None, None, :], suf_scores, FLOOR)
        self_score = jnp.einsum('kgd,kd->kg', query_grid, self_key.astype(jnp.float32).reshape(KVH, DH)) * scale_factor
        suf_peak = jnp.maximum(lax.optimization_barrier(jnp.max(suf_scores, axis=2)), self_score)
        suf_terms = jnp.exp(suf_scores - suf_peak[..., None])
        self_term = jnp.exp(self_score - suf_peak)
        suf_total = lax.optimization_barrier(jnp.sum(suf_terms, axis=2)) + self_term
        suf_weights = lax.optimization_barrier(suf_terms.astype(jnp.bfloat16)).astype(jnp.float32)
        self_weight = lax.optimization_barrier(self_term.astype(jnp.bfloat16)).astype(jnp.float32)
        suf_sum = jnp.einsum('kgt,tkd->kgd', suf_weights, suf_vals)
        suf_sum = suf_sum + self_weight[..., None] * self_value.astype(jnp.float32).reshape(KVH, 1, DH)
        is_home = (jnp.arange(N_CTX, dtype=jnp.int32) == home_id)[None, None, :]
        part_peak = jnp.where(is_home, jnp.maximum(pre_peak, suf_peak[..., None]), pre_peak)
        factor_a = jnp.exp(pre_peak - part_peak)
        factor_b = jnp.where(is_home, jnp.exp(suf_peak[..., None] - part_peak), 0.0)
        part_total = pre_total * factor_a + suf_total[..., None] * factor_b
        part_sum = pre_sum * factor_a[..., None] + suf_sum[:, :, None, :] * factor_b[..., None]
        part_avg = lax.optimization_barrier((part_sum / part_total[..., None]).astype(jnp.bfloat16)).astype(jnp.float32)
        part_mass = part_peak + jnp.log(part_total)
        top = lax.optimization_barrier(jnp.max(part_mass, axis=2))
        share = jnp.exp(part_mass - top[..., None])
        numer = lax.optimization_barrier(jnp.sum(share[..., None] * part_avg, axis=2))
        return (numer / lax.optimization_barrier(jnp.sum(share, axis=2))[..., None]).astype(jnp.bfloat16).reshape(QH * DH)
    attended = lax.map(one_sample, (queries, owners, homes, suffix_lengths, suffix_keys, suffix_values, new_keys, new_values))
    return jnp.dot(attended, out_weight, preferred_element_type=jnp.float32).astype(jnp.bfloat16)
```

```python
import functools
import math

import jax
import jax.numpy as jnp
from jax import lax
from jax.experimental import pallas as pl
from jax.experimental.pallas import tpu as pltpu
from jax.sharding import PartitionSpec as P

QH = 64
KVH = 8
DH = 128
GQ = QH // KVH
FLOOR = -1e30
SCALE = 1.0 / math.sqrt(DH)
MASS_ROWS = 16
ROWS = 16
TILE = ROWS * GQ


def suffix_kernel(len_ref, q_ref, sk_ref, sv_ref, nk_ref, nv_ref, out_ref):
    samp, suf, _ = sk_ref.shape
    rows = GQ * samp
    row_samp = lax.broadcasted_iota(jnp.int32, (rows, suf), 0) % samp
    pos = lax.broadcasted_iota(jnp.int32, (rows, suf), 1)
    for h in range(KVH):
        cols = slice(h * DH, (h + 1) * DH)
        q = q_ref[h]
        scores = []
        for j in range(samp):
            s = lax.dot_general(
                q, sk_ref[j, :, cols], (((1,), (1,)), ((), ())), preferred_element_type=jnp.float32
            )
            seen = (row_samp == j) & (pos < len_ref[j])
            scores.append(jnp.where(seen, s * SCALE, FLOOR))
        own = lax.broadcasted_iota(jnp.int32, (rows, DH), 0) % samp
        nk = jnp.zeros((rows, DH), jnp.float32)
        nv = jnp.zeros((rows, DH), jnp.float32)
        for j in range(samp):
            nk = jnp.where(own == j, nk_ref[j : j + 1, cols].astype(jnp.float32), nk)
            nv = jnp.where(own == j, nv_ref[j : j + 1, cols].astype(jnp.float32), nv)
        self_score = jnp.sum(q.astype(jnp.float32) * nk, axis=1, keepdims=True) * SCALE
        peak = self_score
        for s in scores:
            peak = jnp.maximum(peak, jnp.max(s, axis=1, keepdims=True))
        self_term = jnp.exp(self_score - peak)
        total = self_term
        acc = self_term.astype(jnp.bfloat16).astype(jnp.float32) * nv
        for j in range(samp):
            terms = jnp.exp(scores[j] - peak)
            total = total + jnp.sum(terms, axis=1, keepdims=True)
            acc = acc + jnp.dot(
                terms.astype(jnp.bfloat16), sv_ref[j, :, cols], preferred_element_type=jnp.float32
            )
        out_ref[h, :, 0:DH] = acc
        out_ref[h, :, DH : 2 * DH] = jnp.broadcast_to(peak, (rows, DH))
        out_ref[h, :, 2 * DH : 3 * DH] = jnp.broadcast_to(total, (rows, DH))


def split_mass(mass):
    high = mass.astype(jnp.bfloat16).astype(jnp.float32)
    mid = (mass - high).astype(jnp.bfloat16).astype(jnp.float32)
    return high, mid, mass - high - mid


def mass_block(terms, head):
    lines = [x[head : head + 2] for x in terms]
    return jnp.concatenate(lines + [jnp.zeros((MASS_ROWS - 6, DH), jnp.float32)], axis=0)


def read_mass(ref, rows):
    terms = ref[:, rows:, 0:DH].astype(jnp.float32)
    return terms[:, 0:2] + terms[:, 2:4] + terms[:, 4:6]


def as_columns(x):
    parts, heads, _ = x.shape
    lines = [x[:, h, :] for h in range(heads)]
    return jnp.concatenate(lines + [jnp.zeros((DH - heads * parts, DH), jnp.float32)], axis=0).T


def natural_order(core, rows):
    half = rows // 2
    to = lax.broadcasted_iota(jnp.int32, (rows, rows), 0)
    at = lax.broadcasted_iota(jnp.int32, (rows, rows), 1)
    side = jnp.where(at < half, core, 1 - core)
    local = at % half
    hit = to == 4 * (local // 2) + 2 * side + local % 2
    return hit.astype(jnp.float32).astype(jnp.bfloat16)


def prefix_kernel(
    info_ref, q_own, q_oth, k_ref, v_ref, suf_ref, keep_ref, send_ref, q_ref, acc_ref, peak_ref, total_ref
):
    count = info_ref[0]
    core = info_ref[1]
    home_tile = info_ref[2]
    home_row = info_ref[3]
    tiles = q_ref.shape[0] // ROWS
    positions = k_ref.shape[1]
    contract = (((1,), (1,)), ((), ()))
    both_q = jnp.concatenate([q_own[...], q_oth[...]], axis=0)
    q_ref[...] = jnp.dot(
        natural_order(core, tiles * ROWS), both_q, preferred_element_type=jnp.float32
    ).astype(jnp.bfloat16)
    both = jnp.minimum(count // ROWS, tiles - 1)

    for i in range(tiles):
        if i < tiles - 1:
            prompt = (i >= both).astype(jnp.int32)
            tile = i + prompt
            prompts = [prompt]
        else:
            tile = both
            prompts = [0, 1]
        base = pl.multiple_of(tile * ROWS, ROWS)
        q = jnp.concatenate(
            [q_ref[pl.ds(base, ROWS), g * DH : (g + 1) * DH] for g in range(GQ)], axis=0
        )
        row_samp = lax.broadcasted_iota(jnp.int32, (TILE, positions), 0) % ROWS + base
        s = [
            lax.dot_general(q, k_ref[p], contract, preferred_element_type=jnp.float32)
            for p in prompts
        ]
        s = s[0] if len(s) == 1 else jnp.where(row_samp < count, s[0], s[1])
        peak = jnp.max(s, axis=1, keepdims=True)
        terms = jnp.exp((s - peak) * SCALE)
        total = jnp.sum(terms, axis=1, keepdims=True)
        terms = terms.astype(jnp.bfloat16)
        acc = [jnp.dot(terms, v_ref[p], preferred_element_type=jnp.float32) for p in prompts]
        acc = acc[0] if len(acc) == 1 else jnp.where(row_samp[:, :DH] < count, acc[0], acc[1])
        acc_ref[tile] = acc
        peak_ref[tile] = jnp.broadcast_to(peak * SCALE, (TILE, DH))
        total_ref[tile] = jnp.broadcast_to(total, (TILE, DH))

    row = lax.broadcasted_iota(jnp.int32, (ROWS, DH), 0)
    for g in range(GQ):
        part = slice(g * ROWS, (g + 1) * ROWS)
        add = jnp.zeros((ROWS, DH), jnp.float32)
        add_peak = jnp.full((ROWS, DH), FLOOR, jnp.float32)
        add_total = jnp.zeros((ROWS, DH), jnp.float32)
        for j in range(2):
            here = row == home_row + j
            line = slice(2 * g + j, 2 * g + j + 1)
            add = jnp.where(here, suf_ref[0, line, 0:DH], add)
            add_peak = jnp.where(here, suf_ref[0, line, DH : 2 * DH], add_peak)
            add_total = jnp.where(here, suf_ref[0, line, 2 * DH : 3 * DH], add_total)
        peak = peak_ref[home_tile, part, :]
        top = jnp.maximum(peak, add_peak)
        a = jnp.exp(peak - top)
        b = jnp.exp(add_peak - top)
        acc_ref[home_tile, part, :] = acc_ref[home_tile, part, :] * a + add * b
        total_ref[home_tile, part, :] = total_ref[home_tile, part, :] * a + add_total * b
        peak_ref[home_tile, part, :] = top

    def place(chip, rows, cols, first, second):
        keep_ref[chip, rows, cols] = jnp.where(core == 0, first, second)
        send_ref[chip, rows, cols] = jnp.where(core == 0, second, first).astype(jnp.bfloat16)

    lane = lax.broadcasted_iota(jnp.int32, (ROWS, DH), 1)
    columns = []
    for t in range(tiles):
        column = jnp.zeros((ROWS, DH), jnp.float32)
        avg = []
        for g in range(GQ):
            part = slice(g * ROWS, (g + 1) * ROWS)
            total = total_ref[t, part, :]
            avg.append(acc_ref[t, part, :] / total)
            column = jnp.where(lane == g, peak_ref[t, part, :] + jnp.log(total), column)
        columns.append(column)
        for chip in range(2):
            for h in range(2):
                g = 4 * chip + h
                place(
                    chip,
                    slice(t * ROWS, (t + 1) * ROWS),
                    slice(h * DH, (h + 1) * DH),
                    avg[g],
                    avg[g + 2],
                )
    columns.append(jnp.zeros((DH - tiles * ROWS, DH), jnp.float32))
    terms = split_mass(jnp.concatenate(columns, axis=0).T)
    for chip in range(2):
        blocks = [mass_block(terms, 4 * chip + 2 * side) for side in range(2)]
        place(chip, slice(tiles * ROWS, None), slice(0, DH), *blocks)
        place(chip, slice(tiles * ROWS, None), slice(DH, None), *[jnp.zeros_like(blocks[0])] * 2)


def join_kernel(keep_ref, recv_ref, out_ref):
    parts, rows, width = out_ref.shape
    rows = rows - MASS_ROWS
    heads = width // DH
    masses = [read_mass(ref, rows) for ref in (keep_ref, recv_ref)]
    top = jnp.maximum(*masses)
    shares = [jnp.exp(m - top) for m in masses]
    total = shares[0] + shares[1]
    weights = [as_columns(x / total) for x in shares]
    terms = split_mass((top + jnp.log(total)).reshape(parts * heads, DH))
    for p in range(parts):
        for h in range(heads):
            cols = slice(h * DH, (h + 1) * DH)
            c = h * parts + p
            acc = weights[0][:rows, c : c + 1] * keep_ref[p, :rows, cols]
            acc = acc + weights[1][:rows, c : c + 1] * recv_ref[p, :rows, cols].astype(jnp.float32)
            out_ref[p, :rows, cols] = acc.astype(jnp.bfloat16)
        block = mass_block(terms, heads * p).astype(jnp.bfloat16)
        out_ref[p, rows:, 0:DH] = block
        out_ref[p, rows:, DH:] = jnp.zeros_like(block)


def project_kernel(info_ref, parts_ref, *rest):
    blocks = rest[:8]
    keep_ref, send_ref, w_ref, sems = rest[8:]
    core = info_ref[1]
    copies = [pltpu.make_async_copy(b, w_ref.at[i], sems.at[i]) for i, b in enumerate(blocks)]
    for c in copies:
        c.start()
    parts, rows, width = parts_ref.shape
    rows = rows - MASS_ROWS
    heads = width // DH
    mass = read_mass(parts_ref, rows)
    share = jnp.exp(mass - jnp.max(mass, axis=0, keepdims=True))
    flat = as_columns(share / jnp.sum(share, axis=0, keepdims=True))
    joined = []
    for h in range(heads):
        acc = jnp.zeros((rows, DH), jnp.float32)
        for p in range(parts):
            c = h * parts + p
            acc = acc + flat[:rows, c : c + 1] * parts_ref[p, :rows, h * DH : (h + 1) * DH].astype(
                jnp.float32
            )
        joined.append(acc.astype(jnp.bfloat16))
    attended = jnp.concatenate(joined, axis=1)
    half = rows // 2
    attended = lax.dot_general(
        natural_order(core, rows),
        attended,
        (((0,), (0,)), ((), ())),
        preferred_element_type=jnp.float32,
    ).astype(jnp.bfloat16)
    cols = w_ref.shape[2]
    for i, c in enumerate(copies):
        c.wait()
        out = jnp.dot(attended, w_ref[i], preferred_element_type=jnp.float32)
        at = pl.multiple_of(info_ref[4 + i] * cols, DH)
        keep_ref[:, pl.ds(at, cols)] = out[:half]
        send_ref[:, pl.ds(at, cols)] = out[half:].astype(jnp.bfloat16)


def body(
    queries,
    prefix_keys,
    prefix_values,
    suffix_keys,
    suffix_values,
    new_keys,
    new_values,
    suffix_lengths,
    counts,
    out_weight,
):
    bf16, f32, i32 = jnp.bfloat16, jnp.float32, jnp.int32
    samp = queries.shape[0]
    n_ctx = lax.axis_size("ctx")
    n_grp = lax.axis_size("group")
    chips = n_ctx // 2
    me = lax.axis_index("ctx")
    z = lax.axis_index("group")
    core = me % 2
    row_count = samp * n_ctx
    same_core = [[2 * d + k for d in range(chips)] for k in range(2)]

    def other_core(x):
        return lax.ppermute(x, "ctx", [(i, i ^ 1) for i in range(n_ctx)])

    def after(x, *earlier):
        return lax.optimization_barrier((x,) + earlier)[0]

    def along_z(x, by):
        return lax.ppermute(x, "group", [(i, (i + by) % n_grp) for i in range(n_grp)])

    with jax.named_scope("spread_queries"):
        spread = jnp.broadcast_to(queries[None], (chips,) + queries.shape)
        q_own = lax.all_to_all(spread, "ctx", 0, 0, tiled=True, axis_index_groups=same_core)
        q_own = q_own.reshape(row_count // 2, QH * DH)

    with jax.named_scope("weights"):
        up1, down1 = along_z(out_weight, 1), along_z(out_weight, -1)

    origin = [(z - by) % n_grp for by in (0, 1, -1, 2, -2, 3, -3, 4)]
    info = jnp.stack(
        [counts[0].astype(i32), core, (samp * me) // ROWS, (samp * me) % ROWS] + origin
    ).astype(i32)

    vmem = pl.BlockSpec(memory_space=pltpu.VMEM)
    smem = pl.BlockSpec(memory_space=pltpu.SMEM)
    with jax.named_scope("suffix"):
        own_q = queries.reshape(samp, KVH, GQ, DH).transpose(1, 2, 0, 3).reshape(KVH, GQ * samp, DH)
        suffix = pl.pallas_call(
            suffix_kernel,
            out_shape=jax.ShapeDtypeStruct((KVH, GQ * samp, 3 * DH), f32),
            in_specs=[smem] + [vmem] * 5,
            out_specs=vmem,
            compiler_params=pltpu.CompilerParams(vmem_limit_bytes=24 * 2**20),
            cost_estimate=pl.CostEstimate(
                flops=2**27, bytes_accessed=2**21, transcendentals=2**16
            ),
        )(suffix_lengths, own_q, suffix_keys, suffix_values, new_keys, new_values)

    with jax.named_scope("weights"):
        up2, down2 = along_z(after(up1, suffix), 1), along_z(after(down1, suffix), -1)

    with jax.named_scope("spread_queries"):
        q_oth = other_core(after(q_own, suffix, up1, down1))

    with jax.named_scope("prefix"):
        prompts, positions, _ = prefix_keys.shape
        sent_rows = row_count + MASS_ROWS
        tiles = row_count // ROWS
        q_block = pl.BlockSpec((row_count // 2, GQ * DH), lambda j, info: (0, j))
        kv_block = pl.BlockSpec((prompts, positions, DH), lambda j, info: (0, 0, j))
        suf_block = pl.BlockSpec((1, GQ * samp, 3 * DH), lambda j, info: (j, 0, 0))
        out_block = pl.BlockSpec((2, sent_rows, 2 * DH), lambda j, info: (j, 0, 0))
        keep, send = pl.pallas_call(
            prefix_kernel,
            out_shape=(
                jax.ShapeDtypeStruct((chips, sent_rows, 2 * DH), f32),
                jax.ShapeDtypeStruct((chips, sent_rows, 2 * DH), bf16),
            ),
            grid_spec=pltpu.PrefetchScalarGridSpec(
                num_scalar_prefetch=1,
                grid=(KVH,),
                in_specs=[q_block, q_block, kv_block, kv_block, suf_block],
                out_specs=(out_block, out_block),
                scratch_shapes=[pltpu.VMEM((row_count, GQ * DH), bf16)]
                + [pltpu.VMEM((tiles, TILE, DH), f32)] * 3,
            ),
            compiler_params=pltpu.CompilerParams(vmem_limit_bytes=56 * 2**20),
            cost_estimate=pl.CostEstimate(
                flops=3 * 2**30, bytes_accessed=9 * 2**20, transcendentals=2**22
            ),
        )(info, q_own, q_oth, prefix_keys, prefix_values, suffix)

    with jax.named_scope("join_cores"):
        parts = pl.pallas_call(
            join_kernel,
            out_shape=jax.ShapeDtypeStruct((chips, sent_rows, 2 * DH), bf16),
            in_specs=[vmem, vmem],
            out_specs=vmem,
            compiler_params=pltpu.CompilerParams(vmem_limit_bytes=24 * 2**20),
        )(keep, other_core(send))

    with jax.named_scope("weights"):
        up3, down3 = along_z(after(up2, send), 1), along_z(after(down2, send), -1)
        up4 = along_z(up3, 1)
        blocks = (out_weight, up1, down1, up2, down2, up3, down3, up4)

    with jax.named_scope("send_parts"):
        parts = lax.all_to_all(parts, "ctx", 0, 0, tiled=True, axis_index_groups=same_core)

    with jax.named_scope("project"):
        width = out_weight.shape[1]
        keep, send = pl.pallas_call(
            project_kernel,
            out_shape=(
                jax.ShapeDtypeStruct((row_count // 2, n_grp * width), f32),
                jax.ShapeDtypeStruct((row_count // 2, n_grp * width), bf16),
            ),
            in_specs=[smem, vmem] + [pl.BlockSpec(memory_space=pl.ANY)] * len(blocks),
            out_specs=(vmem, vmem),
            scratch_shapes=[
                pltpu.VMEM((len(blocks),) + out_weight.shape, bf16),
                pltpu.SemaphoreType.DMA((len(blocks),)),
            ],
            compiler_params=pltpu.CompilerParams(vmem_limit_bytes=24 * 2**20),
            cost_estimate=pl.CostEstimate(
                flops=2**28, bytes_accessed=2**22, transcendentals=2**12
            ),
        )(info, parts, *blocks)

    with jax.named_scope("send_rows"):
        got = other_core(send)
        rows = (keep + got.astype(f32)).astype(bf16).reshape(chips, samp, n_grp * width)
        rows = lax.all_to_all(rows, "ctx", 0, 0, tiled=True, axis_index_groups=same_core)
        return jnp.sum(rows.astype(f32), axis=0).astype(bf16)


def solution(mesh):
    in_specs = (
        P(("group", "ctx"), None),
        P("group", "ctx", None),
        P("group", "ctx", None),
        P(("group", "ctx"), None, None),
        P(("group", "ctx"), None, None),
        P(("group", "ctx"), None),
        P(("group", "ctx"), None),
        P(("group", "ctx")),
        P("group"),
        P("ctx", "group"),
    )
    out_specs = P(("group", "ctx"), None)
    return jax.shard_map(body, mesh=mesh, in_specs=in_specs, out_specs=out_specs, check_vma=False)
```

```python
import math

import jax
import jax.numpy as jnp
import numpy as np
from jax import lax
from jax.experimental import pallas as pl
from jax.experimental.pallas import tpu as pltpu
from jax.sharding import PartitionSpec as P

QH = 64
KVH = 8
DH = 128
GQ = QH // KVH
CHIP_HEADS = 4
WIDE = CHIP_HEADS * DH
SENT = WIDE + DH
FLOOR = -1e30
SCALE = 1.0 / math.sqrt(DH)
ROWS = 16
TILE = ROWS * GQ
SPLITS = (5, 3)
CONTRACT = (((1,), (1,)), ((), ()))


def suffix_kernel(len_ref, q_hbm, sk_hbm, sv_hbm, nk_hbm, nv_hbm, out_ref, q_ref, sk_ref, sv_ref, nk_ref, nv_ref, sems):
    pairs = (
        (q_hbm, q_ref),
        (nk_hbm, nk_ref),
        (nv_hbm, nv_ref),
        (sk_hbm, sk_ref),
        (sv_hbm, sv_ref),
    )
    copies = [pltpu.make_async_copy(a, b, sems.at[i]) for i, (a, b) in enumerate(pairs)]
    for c in copies:
        c.start()
    for c in copies:
        c.wait()
    samp, suf, _ = sk_ref.shape
    rows = GQ * samp
    row_samp = lax.broadcasted_iota(jnp.int32, (rows, suf), 0) % samp
    pos = lax.broadcasted_iota(jnp.int32, (rows, suf), 1)
    own = lax.broadcasted_iota(jnp.int32, (rows, DH), 0) % samp
    for h in range(KVH):
        cols = slice(h * DH, (h + 1) * DH)
        q = jnp.concatenate(
            [
                q_ref[:, (h * GQ + g) * DH : (h * GQ + g + 1) * DH].astype(jnp.float32)
                for g in range(GQ)
            ],
            axis=0,
        )
        q16 = q.astype(jnp.bfloat16)
        scores = []
        for j in range(samp):
            s = lax.dot_general(
                q16, sk_ref[j, :, cols], CONTRACT, preferred_element_type=jnp.float32
            )
            seen = (row_samp == j) & (pos < len_ref[j])
            scores.append(jnp.where(seen, s * SCALE, FLOOR))
        nk = jnp.zeros((rows, DH), jnp.float32)
        nv = jnp.zeros((rows, DH), jnp.float32)
        for j in range(samp):
            nk = jnp.where(own == j, nk_ref[j : j + 1, cols].astype(jnp.float32), nk)
            nv = jnp.where(own == j, nv_ref[j : j + 1, cols].astype(jnp.float32), nv)
        self_score = jnp.sum(q * nk, axis=1, keepdims=True) * SCALE
        peak = self_score
        for s in scores:
            peak = jnp.maximum(peak, jnp.max(s, axis=1, keepdims=True))
        self_term = jnp.exp(self_score - peak)
        total = self_term
        acc = self_term.astype(jnp.bfloat16).astype(jnp.float32) * nv
        for j in range(samp):
            terms = jnp.exp(scores[j] - peak)
            total = total + jnp.sum(terms, axis=1, keepdims=True)
            acc = acc + jnp.dot(
                terms.astype(jnp.bfloat16), sv_ref[j, :, cols], preferred_element_type=jnp.float32
            )
        out_ref[h, :, 0:DH] = acc
        out_ref[h, :, DH : 2 * DH] = jnp.broadcast_to(peak, (rows, DH))
        out_ref[h, :, 2 * DH : 3 * DH] = jnp.broadcast_to(total, (rows, DH))


def spread_kernel(q_ref, out_ref):
    for d in range(out_ref.shape[0]):
        out_ref[d] = q_ref[...]


def mass_block(mass, rows):
    high = mass.astype(jnp.bfloat16).astype(jnp.float32)
    mid = (mass - high).astype(jnp.bfloat16).astype(jnp.float32)
    row = lax.broadcasted_iota(jnp.int32, (rows, DH), 0)
    block = jnp.where(row == 0, high, jnp.where(row == 1, mid, mass - high - mid))
    return jnp.where(row < 3, block, 0.0)


def read_mass(ref):
    block = ref[:, 0:16, WIDE:].astype(jnp.float32)
    return block[:, 0] + block[:, 1] + block[:, 2]


def as_columns(x):
    parts = x.shape[0]
    return jnp.concatenate([x, jnp.zeros((DH - parts, DH), jnp.float32)], axis=0).T


def prefix_kernel(
    info_ref,
    counts_ref,
    q_own,
    q_oth,
    k_ref,
    v_ref,
    suf_ref,
    keep_ref,
    send_ref,
    acc_ref,
    peak_ref,
    total_ref,
):
    core = info_ref[0]
    positions = k_ref.shape[1]
    rows = q_own.shape[0]
    tiles = rows // ROWS
    visits = []
    for side, q_ref in enumerate((q_own, q_oth)):
        left = jnp.maximum(counts_ref[0] - 2 * (core if side == 0 else 1 - core), 0)
        count = 2 * (left // 4) + jnp.minimum(left % 4, 2)
        both = jnp.minimum(count // ROWS, tiles - 1)
        for i in range(tiles - 1):
            prompt = (i >= both).astype(jnp.int32)
            visits.append((side, q_ref, i + prompt, [prompt], count))
        visits.append((side, q_ref, both, [0, 1], count))

    def scores(visit):
        _, q_ref, tile, prompts, count = visit
        base = pl.multiple_of(tile * ROWS, ROWS)
        q = jnp.concatenate(
            [q_ref[pl.ds(base, ROWS), g * DH : (g + 1) * DH] for g in range(GQ)], axis=0
        )
        s = [
            lax.dot_general(q, k_ref[p], CONTRACT, preferred_element_type=jnp.float32)
            for p in prompts
        ]
        if len(s) == 1:
            return s[0]
        row = lax.broadcasted_iota(jnp.int32, (TILE, positions), 0) % ROWS + base
        return jnp.where(row < count, s[0], s[1])

    ahead = scores(visits[0])
    for i, (side, _, tile, prompts, count) in enumerate(visits):
        s = ahead
        if i + 1 < len(visits):
            ahead = scores(visits[i + 1])
        peak = jnp.max(s, axis=1, keepdims=True)
        terms = jnp.exp((s - peak) * SCALE)
        total = jnp.sum(terms, axis=1, keepdims=True)
        terms = terms.astype(jnp.bfloat16)
        acc = [jnp.dot(terms, v_ref[p], preferred_element_type=jnp.float32) for p in prompts]
        if len(acc) == 2:
            row = lax.broadcasted_iota(jnp.int32, (TILE, DH), 0) % ROWS + tile * ROWS
            acc = [jnp.where(row < count, acc[0], acc[1])]
        at = side * tiles + tile
        acc_ref[at] = acc[0]
        peak_ref[at] = jnp.broadcast_to(peak * SCALE, (TILE, DH))
        total_ref[at] = jnp.broadcast_to(total, (TILE, DH))

    home_tile = info_ref[1]
    home_row = info_ref[2]
    row = lax.broadcasted_iota(jnp.int32, (ROWS, DH), 0)
    for g in range(GQ):
        part = slice(g * ROWS, (g + 1) * ROWS)
        add = jnp.zeros((ROWS, DH), jnp.float32)
        add_peak = jnp.full((ROWS, DH), FLOOR, jnp.float32)
        add_total = jnp.zeros((ROWS, DH), jnp.float32)
        for j in range(2):
            here = row == home_row + j
            line = slice(2 * g + j, 2 * g + j + 1)
            add = jnp.where(here, suf_ref[0, line, 0:DH], add)
            add_peak = jnp.where(here, suf_ref[0, line, DH : 2 * DH], add_peak)
            add_total = jnp.where(here, suf_ref[0, line, 2 * DH : 3 * DH], add_total)
        peak = peak_ref[home_tile, part, :]
        top = jnp.maximum(peak, add_peak)
        a = jnp.exp(peak - top)
        b = jnp.exp(add_peak - top)
        acc_ref[home_tile, part, :] = acc_ref[home_tile, part, :] * a + add * b
        total_ref[home_tile, part, :] = total_ref[home_tile, part, :] * a + add_total * b
        peak_ref[home_tile, part, :] = top

    lane = lax.broadcasted_iota(jnp.int32, (ROWS, DH), 1)
    lines = [[None] * (CHIP_HEADS * tiles) for _ in range(4)]
    for side, out_ref in enumerate((keep_ref, send_ref)):
        for t in range(tiles):
            for g in range(GQ):
                chip, h = g // CHIP_HEADS, g % CHIP_HEADS
                part = slice(g * ROWS, (g + 1) * ROWS)
                total = total_ref[side * tiles + t, part, :]
                avg = acc_ref[side * tiles + t, part, :] / total
                out_ref[chip, t * ROWS : (t + 1) * ROWS, h * DH : (h + 1) * DH] = avg.astype(
                    out_ref.dtype
                )
                lines[2 * side + chip][h * tiles + t] = peak_ref[
                    side * tiles + t, part, :
                ] + jnp.log(total)
    table = []
    for i in range(CHIP_HEADS * tiles):
        block = lines[0][i]
        for c in range(1, 4):
            block = jnp.where(lane == c, lines[c][i], block)
        table.append(block)
    table = jnp.concatenate(table, axis=0).T
    for side, out_ref in enumerate((keep_ref, send_ref)):
        for chip in range(2):
            c = 2 * side + chip
            out_ref[chip, :, WIDE:] = mass_block(table[c : c + 1], rows).astype(out_ref.dtype)


def join_kernel(*refs):
    out_ref = refs[-1]
    calls = len(SPLITS)
    at = 0
    for keep_ref, recv_ref in zip(refs[:calls], refs[calls : 2 * calls]):
        parts, rows, _ = keep_ref.shape
        masses = [read_mass(ref) for ref in (keep_ref, recv_ref)]
        top = jnp.maximum(*masses)
        shares = [jnp.exp(m - top) for m in masses]
        total = shares[0] + shares[1]
        weights = [as_columns(x / total) for x in shares]
        mass = top + jnp.log(total)
        for p in range(parts):
            for h in range(CHIP_HEADS):
                cols = slice(h * DH, (h + 1) * DH)
                a, b = [w[h * rows : (h + 1) * rows, p : p + 1] for w in weights]
                acc = a * keep_ref[p, :, cols] + b * recv_ref[p, :, cols].astype(jnp.float32)
                out_ref[at + p, :, cols] = acc.astype(jnp.bfloat16)
            block = mass_block(mass[p : p + 1], rows)
            out_ref[at + p, :, WIDE:] = block.astype(jnp.bfloat16)
        at += parts


def project_kernel(info_ref, parts_ref, *rest):
    blocks, out_ref = rest[:-1], rest[-1]
    core = info_ref[0]
    parts, rows, _ = parts_ref.shape
    mass = read_mass(parts_ref)
    share = jnp.exp(mass - jnp.max(mass, axis=0, keepdims=True))
    flat = as_columns(share / jnp.sum(share, axis=0, keepdims=True))
    heads = []
    for h in range(CHIP_HEADS):
        acc = jnp.zeros((rows, DH), jnp.float32)
        for p in range(parts):
            acc = acc + flat[h * rows : (h + 1) * rows, p : p + 1] * parts_ref[
                p, :, h * DH : (h + 1) * DH
            ].astype(jnp.float32)
        heads.append(acc)
    half = CHIP_HEADS // 2
    first = jnp.concatenate(heads[:half], axis=1)
    second = jnp.concatenate(heads[half:], axis=1)
    own = jnp.where(core == 0, first, second).astype(jnp.bfloat16)
    oth = jnp.where(core == 0, second, first).astype(jnp.bfloat16)
    own_first = jnp.concatenate([own, oth], axis=1)
    oth_first = jnp.concatenate([oth, own], axis=1)
    cols = blocks[0].shape[1]
    plan = [((own, blocks[0]), (oth, blocks[1]))]
    plan += [((oth_first if i in (1, 3, 5) else own_first, b),) for i, b in enumerate(blocks[2:])]
    for i, terms in enumerate(plan):
        out = sum(jnp.dot(a, w[...], preferred_element_type=jnp.float32) for a, w in terms)
        to = pl.multiple_of(info_ref[3 + i] * cols, DH)
        for chip in range(out_ref.shape[0]):
            out_ref[chip, :, pl.ds(to, cols)] = out[2 * chip : 2 * chip + 2].astype(jnp.bfloat16)


def body(
    queries,
    prefix_keys,
    prefix_values,
    suffix_keys,
    suffix_values,
    new_keys,
    new_values,
    suffix_lengths,
    counts,
    out_weight,
):
    bf16, f32, i32 = jnp.bfloat16, jnp.float32, jnp.int32
    samp = queries.shape[0]
    n_ctx = lax.axis_size("ctx")
    n_grp = lax.axis_size("group")
    chips = n_ctx // 2
    me = lax.axis_index("ctx")
    z = lax.axis_index("group")
    rows = samp * chips
    same_core = [[2 * d + k for d in range(chips)] for k in range(2)]
    ring = [
        (g * n_ctx + c, (g + (1 if c % 2 == 0 else -1)) % n_grp * n_ctx + c)
        for g in range(n_grp)
        for c in range(n_ctx)
    ]

    def other_core(x):
        return lax.ppermute(x, "ctx", [(i, i ^ 1) for i in range(n_ctx)])

    def along_z(x):
        return lax.ppermute(x, ("group", "ctx"), ring)

    def after(x, *earlier):
        return lax.optimization_barrier((x,) + earlier)[0]

    vmem = pl.BlockSpec(memory_space=pltpu.VMEM)
    smem = pl.BlockSpec(memory_space=pltpu.SMEM)
    hbm = pl.BlockSpec(memory_space=pl.ANY)

    with jax.named_scope("spread_queries"):
        spread = pl.pallas_call(
            spread_kernel,
            out_shape=jax.ShapeDtypeStruct((chips,) + queries.shape, bf16),
            in_specs=[vmem],
            out_specs=vmem,
            cost_estimate=pl.CostEstimate(flops=1, bytes_accessed=2**19, transcendentals=0),
        )(queries)
        q_own = lax.all_to_all(spread, "ctx", 0, 0, tiled=True, axis_index_groups=same_core)
        q_own = q_own.reshape(rows, QH * DH)

    with jax.named_scope("weights"):
        w_oth = other_core(out_weight)
        x1_own = along_z(out_weight)
        x1_oth = along_z(w_oth)

    table = []
    for g in range(n_grp):
        for c in range(n_ctx):
            way = 1 - 2 * (c % 2)
            home = samp * (c // 2)
            origin = [(g - way * by) % n_grp for by in (0, 1, -1, 2, -2, 3, -3, 4)]
            table.append([c % 2, home // ROWS, home % ROWS] + origin)
    info = lax.dynamic_index_in_dim(
        jnp.asarray(np.array(table, np.int32)), z * n_ctx + me, 0, keepdims=False
    )

    with jax.named_scope("suffix"):
        given = (queries, suffix_keys, suffix_values, new_keys, new_values)
        suffix = pl.pallas_call(
            suffix_kernel,
            out_shape=jax.ShapeDtypeStruct((KVH, GQ * samp, 3 * DH), f32),
            in_specs=[smem] + [hbm] * 5,
            out_specs=vmem,
            scratch_shapes=[pltpu.VMEM(x.shape, x.dtype) for x in given]
            + [pltpu.SemaphoreType.DMA((5,))],
            compiler_params=pltpu.CompilerParams(vmem_limit_bytes=56 * 2**20),
            cost_estimate=pl.CostEstimate(flops=1, bytes_accessed=1, transcendentals=1),
        )(suffix_lengths, *given)

    with jax.named_scope("weights"):
        x1 = jnp.concatenate([x1_own, x1_oth], axis=0)

    with jax.named_scope("spread_queries"):
        q_oth = other_core(after(q_own, suffix, x1))

    with jax.named_scope("weights"):
        q_oth, x1 = lax.optimization_barrier((q_oth, x1))
        x2 = along_z(x1)
        e1 = other_core(x1)

    keeps, recvs = [], []
    with jax.named_scope("prefix"):
        prompts, positions, _ = prefix_keys.shape
        tiles = 2 * rows // ROWS
        for n, heads in enumerate(SPLITS):
            at = sum(SPLITS[:n])
            q_block = pl.BlockSpec((rows, GQ * DH), lambda j, at=at: (0, at + j))
            kv_block = pl.BlockSpec(
                (prompts, positions, DH), lambda j, at=at: (0, 0, at + j)
            )
            suf_block = pl.BlockSpec(
                (1, GQ * samp, 3 * DH), lambda j, at=at: (at + j, 0, 0)
            )
            out_block = pl.BlockSpec((2, rows, SENT), lambda j: (j, 0, 0))
            keep, send = pl.pallas_call(
                prefix_kernel,
                out_shape=(
                    jax.ShapeDtypeStruct((2 * heads, rows, SENT), f32),
                    jax.ShapeDtypeStruct((2 * heads, rows, SENT), bf16),
                ),
                grid=(heads,),
                in_specs=[smem, smem, q_block, q_block, kv_block, kv_block, suf_block],
                out_specs=(out_block, out_block),
                scratch_shapes=[pltpu.VMEM((tiles, TILE, DH), f32)] * 3,
                compiler_params=pltpu.CompilerParams(vmem_limit_bytes=52 * 2**20),
                cost_estimate=pl.CostEstimate(
                    flops=2**31, bytes_accessed=2**23, transcendentals=2**22
                ),
            )(info, counts, q_own, q_oth, prefix_keys, prefix_values, suffix)
            keeps.append(keep)
            if n == 0:
                q_own, q_oth, x2, e1, send = lax.optimization_barrier(
                    (q_own, q_oth, x2, e1, send)
                )
            recvs.append(other_core(send))

    with jax.named_scope("weights"):
        x3 = along_z(x2)
        e2 = other_core(x2)

    with jax.named_scope("join_cores"):
        parts = pl.pallas_call(
            join_kernel,
            out_shape=jax.ShapeDtypeStruct((chips, rows, SENT), bf16),
            in_specs=[vmem] * (2 * len(SPLITS)),
            out_specs=vmem,
            compiler_params=pltpu.CompilerParams(vmem_limit_bytes=24 * 2**20),
        )(*keeps, *recvs)

    with jax.named_scope("weights"):
        parts, x3, e2 = lax.optimization_barrier((parts, x3, e2))
        e3 = other_core(x3)
        x4 = along_z(x3)
        blocks = (out_weight, w_oth, x1, e1, x2, e2, x3, e3, x4)

    with jax.named_scope("send_parts"):
        parts = lax.all_to_all(parts, "ctx", 0, 0, tiled=True, axis_index_groups=same_core)

    with jax.named_scope("project"):
        width = out_weight.shape[1]
        out = pl.pallas_call(
            project_kernel,
            out_shape=jax.ShapeDtypeStruct((chips, samp, n_grp * width), bf16),
            in_specs=[smem] + [vmem] * (1 + len(blocks)),
            out_specs=vmem,
            compiler_params=pltpu.CompilerParams(vmem_limit_bytes=20 * 2**20),
            cost_estimate=pl.CostEstimate(
                flops=2**28, bytes_accessed=2**23, transcendentals=2**12
            ),
        )(info, parts, *blocks)

    with jax.named_scope("send_rows"):
        out = lax.all_to_all(out, "ctx", 0, 0, tiled=True, axis_index_groups=same_core)
        return jnp.sum(out.astype(f32), axis=0).astype(bf16)


def solution(mesh):
    in_specs = (
        P(("group", "ctx"), None),
        P("group", "ctx", None),
        P("group", "ctx", None),
        P(("group", "ctx"), None, None),
        P(("group", "ctx"), None, None),
        P(("group", "ctx"), None),
        P(("group", "ctx"), None),
        P(("group", "ctx")),
        P("group"),
        P("ctx", "group"),
    )
    out_specs = P(("group", "ctx"), None)
    return jax.shard_map(body, mesh=mesh, in_specs=in_specs, out_specs=out_specs, check_vma=False)
```

```python
import math

import jax
import jax.numpy as jnp
import numpy as np
from jax import lax
from jax.experimental import pallas as pl
from jax.experimental.pallas import tpu as pltpu
from jax.sharding import PartitionSpec as P

QH = 64
KVH = 8
DH = 128
GQ = QH // KVH
CHIP_HEADS = 4
MASS_ROWS = 16
FLOOR = -1e30
SCALE = 1.0 / math.sqrt(DH)
ROWS = 16
TILE = ROWS * GQ
SPLITS = (5, 3)
CONTRACT = (((1,), (1,)), ((), ()))


def suffix_kernel(len_ref, info_ref, q_hbm, sk_hbm, sv_hbm, nk_hbm, nv_hbm, out_ref, q_ref, sk_ref, sv_ref, nk_ref, nv_ref, sems):
    pairs = (
        (q_hbm, q_ref),
        (nk_hbm, nk_ref),
        (nv_hbm, nv_ref),
        (sk_hbm, sk_ref),
        (sv_hbm, sv_ref),
    )
    copies = [pltpu.make_async_copy(a, b, sems.at[i]) for i, (a, b) in enumerate(pairs)]
    for c in copies:
        c.start()
    for c in copies:
        c.wait()
    samp, suf, _ = sk_ref.shape
    rows = GQ * samp
    row_samp = lax.broadcasted_iota(jnp.int32, (rows, suf), 0) % samp
    pos = lax.broadcasted_iota(jnp.int32, (rows, suf), 1)
    own = lax.broadcasted_iota(jnp.int32, (rows, DH), 0) % samp
    for h in range(KVH):
        cols = slice(h * DH, (h + 1) * DH)
        q = jnp.concatenate(
            [
                q_ref[:, (h * GQ + g) * DH : (h * GQ + g + 1) * DH].astype(jnp.float32)
                for g in range(GQ)
            ],
            axis=0,
        )
        q16 = q.astype(jnp.bfloat16)
        scores = []
        for j in range(samp):
            s = lax.dot_general(
                q16, sk_ref[j, :, cols], CONTRACT, preferred_element_type=jnp.float32
            )
            seen = (row_samp == j) & (pos < len_ref[j])
            scores.append(jnp.where(seen, s * SCALE, FLOOR))
        nk = jnp.zeros((rows, DH), jnp.float32)
        nv = jnp.zeros((rows, DH), jnp.float32)
        for j in range(samp):
            nk = jnp.where(own == j, nk_ref[j : j + 1, cols].astype(jnp.float32), nk)
            nv = jnp.where(own == j, nv_ref[j : j + 1, cols].astype(jnp.float32), nv)
        self_score = jnp.sum(q * nk, axis=1, keepdims=True) * SCALE
        peak = self_score
        for s in scores:
            peak = jnp.maximum(peak, jnp.max(s, axis=1, keepdims=True))
        self_term = jnp.exp(self_score - peak)
        total = self_term
        acc = self_term.astype(jnp.bfloat16).astype(jnp.float32) * nv
        for j in range(samp):
            terms = jnp.exp(scores[j] - peak)
            total = total + jnp.sum(terms, axis=1, keepdims=True)
            acc = acc + jnp.dot(
                terms.astype(jnp.bfloat16), sv_ref[j, :, cols], preferred_element_type=jnp.float32
            )
        out_ref[h, :, 0:DH] = acc
        out_ref[h, :, DH : 2 * DH] = jnp.broadcast_to(peak, (rows, DH))
        out_ref[h, :, 2 * DH : 3 * DH] = jnp.broadcast_to(total, (rows, DH))


def spread_kernel(q_ref, out_ref):
    for d in range(out_ref.shape[0]):
        out_ref[d] = q_ref[...]


def mass_block(mass, rows):
    high = mass.astype(jnp.bfloat16).astype(jnp.float32)
    mid = (mass - high).astype(jnp.bfloat16).astype(jnp.float32)
    row = lax.broadcasted_iota(jnp.int32, (rows, DH), 0)
    block = jnp.where(row == 0, high, jnp.where(row == 1, mid, mass - high - mid))
    return jnp.where(row < 3, block, 0.0)


def read_mass(ref):
    block = ref[:, ref.shape[1] - MASS_ROWS :, :].astype(jnp.float32)
    return block[:, 0] + block[:, 1] + block[:, 2]


def as_columns(x):
    parts = x.shape[0]
    return jnp.concatenate([x, jnp.zeros((DH - parts, DH), jnp.float32)], axis=0).T


def prefix_kernel(
    info_ref,
    counts_ref,
    q_own,
    q_oth,
    k_ref,
    v_ref,
    suf_ref,
    keep_ref,
    send_ref,
    acc_ref,
    peak_ref,
    total_ref,
):
    core = info_ref[0]
    positions = k_ref.shape[1]
    rows = q_own.shape[0]
    tiles = rows // ROWS
    visits = []
    for side, q_ref in enumerate((q_own, q_oth)):
        left = jnp.maximum(counts_ref[0] - 2 * (core if side == 0 else 1 - core), 0)
        count = 2 * (left // 4) + jnp.minimum(left % 4, 2)
        both = jnp.minimum(count // ROWS, tiles - 1)
        for i in range(tiles - 1):
            prompt = (i >= both).astype(jnp.int32)
            visits.append((side, q_ref, i + prompt, [prompt], count))
        visits.append((side, q_ref, both, [0, 1], count))

    def scores(visit):
        _, q_ref, tile, prompts, count = visit
        base = pl.multiple_of(tile * ROWS, ROWS)
        q = jnp.concatenate(
            [q_ref[pl.ds(base, ROWS), g * DH : (g + 1) * DH] for g in range(GQ)], axis=0
        )
        s = [
            lax.dot_general(q, k_ref[p], CONTRACT, preferred_element_type=jnp.float32)
            for p in prompts
        ]
        if len(s) == 1:
            return s[0]
        row = lax.broadcasted_iota(jnp.int32, (TILE, positions), 0) % ROWS + base
        return jnp.where(row < count, s[0], s[1])

    def weights(s, peak):
        terms = jnp.exp((s - peak) * SCALE)
        return terms.astype(jnp.bfloat16), peak, jnp.sum(terms, axis=1, keepdims=True)

    def values(visit, terms, peak, total):
        side, _, tile, prompts, count = visit
        acc = [jnp.dot(terms, v_ref[p], preferred_element_type=jnp.float32) for p in prompts]
        if len(acc) == 2:
            row = lax.broadcasted_iota(jnp.int32, (TILE, DH), 0) % ROWS + tile * ROWS
            acc = [jnp.where(row < count, acc[0], acc[1])]
        at = side * tiles + tile
        acc_ref[at] = acc[0]
        peak_ref[at] = jnp.broadcast_to(peak * SCALE, (TILE, DH))
        total_ref[at] = jnp.broadcast_to(total, (TILE, DH))

    def scored(visit):
        s = scores(visit)
        return s, jnp.max(s, axis=1, keepdims=True)

    ahead = scored(visits[0])
    behind = None
    for i, visit in enumerate(visits):
        now = ahead
        if i + 1 < len(visits):
            ahead = scored(visits[i + 1])
        if behind is not None:
            values(*behind)
        behind = (visit,) + weights(*now)
    values(*behind)

    home_tile = info_ref[1]
    home_row = info_ref[2]
    row = lax.broadcasted_iota(jnp.int32, (ROWS, DH), 0)
    for g in range(GQ):
        part = slice(g * ROWS, (g + 1) * ROWS)
        add = jnp.zeros((ROWS, DH), jnp.float32)
        add_peak = jnp.full((ROWS, DH), FLOOR, jnp.float32)
        add_total = jnp.zeros((ROWS, DH), jnp.float32)
        for j in range(2):
            here = row == home_row + j
            line = slice(2 * g + j, 2 * g + j + 1)
            add = jnp.where(here, suf_ref[0, line, 0:DH], add)
            add_peak = jnp.where(here, suf_ref[0, line, DH : 2 * DH], add_peak)
            add_total = jnp.where(here, suf_ref[0, line, 2 * DH : 3 * DH], add_total)
        peak = peak_ref[home_tile, part, :]
        top = jnp.maximum(peak, add_peak)
        a = jnp.exp(peak - top)
        b = jnp.exp(add_peak - top)
        acc_ref[home_tile, part, :] = acc_ref[home_tile, part, :] * a + add * b
        total_ref[home_tile, part, :] = total_ref[home_tile, part, :] * a + add_total * b
        peak_ref[home_tile, part, :] = top

    lane = lax.broadcasted_iota(jnp.int32, (ROWS, DH), 1)
    lines = [[None] * (CHIP_HEADS * tiles) for _ in range(4)]
    for side, out_ref in enumerate((keep_ref, send_ref)):
        for t in range(tiles):
            for g in range(GQ):
                chip, h = g // CHIP_HEADS, g % CHIP_HEADS
                part = slice(g * ROWS, (g + 1) * ROWS)
                total = total_ref[side * tiles + t, part, :]
                avg = acc_ref[side * tiles + t, part, :] / total
                at = h * rows + t * ROWS
                out_ref[chip, at : at + ROWS, :] = avg.astype(out_ref.dtype)
                lines[2 * side + chip][h * tiles + t] = peak_ref[
                    side * tiles + t, part, :
                ] + jnp.log(total)
    table = []
    for i in range(CHIP_HEADS * tiles):
        block = lines[0][i]
        for c in range(1, 4):
            block = jnp.where(lane == c, lines[c][i], block)
        table.append(block)
    table = jnp.concatenate(table, axis=0).T
    for side, out_ref in enumerate((keep_ref, send_ref)):
        for chip in range(2):
            c = 2 * side + chip
            block = mass_block(table[c : c + 1], MASS_ROWS)
            out_ref[chip, CHIP_HEADS * rows :, :] = block.astype(out_ref.dtype)


def join_kernel(*refs):
    out_ref = refs[-1]
    calls = len(SPLITS)
    at = 0
    for keep_ref, recv_ref in zip(refs[:calls], refs[calls : 2 * calls]):
        parts = keep_ref.shape[0]
        lines = keep_ref.shape[1] - MASS_ROWS
        masses = [read_mass(ref) for ref in (keep_ref, recv_ref)]
        top = jnp.maximum(*masses)
        shares = [jnp.exp(m - top) for m in masses]
        total = shares[0] + shares[1]
        weights = [as_columns(x / total) for x in shares]
        mass = top + jnp.log(total)
        for p in range(parts):
            a, b = [w[:, p : p + 1] for w in weights]
            acc = a * keep_ref[p, :lines, :] + b * recv_ref[p, :lines, :].astype(jnp.float32)
            out_ref[at + p, :lines, :] = acc.astype(jnp.bfloat16)
            block = mass_block(mass[p : p + 1], MASS_ROWS)
            out_ref[at + p, lines:, :] = block.astype(jnp.bfloat16)
        at += parts


def project_kernel(info_ref, parts_ref, *rest):
    blocks, out_ref = rest[:-1], rest[-1]
    core = info_ref[0]
    parts = parts_ref.shape[0]
    lines = parts_ref.shape[1] - MASS_ROWS
    rows = lines // CHIP_HEADS
    mass = read_mass(parts_ref)
    share = jnp.exp(mass - jnp.max(mass, axis=0, keepdims=True))
    flat = as_columns(share / jnp.sum(share, axis=0, keepdims=True))
    acc = jnp.zeros((lines, DH), jnp.float32)
    for p in range(parts):
        acc = acc + flat[:, p : p + 1] * parts_ref[p, :lines, :].astype(jnp.float32)
    heads = [acc[h * rows : (h + 1) * rows] for h in range(CHIP_HEADS)]
    half = CHIP_HEADS // 2
    first = jnp.concatenate(heads[:half], axis=1)
    second = jnp.concatenate(heads[half:], axis=1)
    own = jnp.where(core == 0, first, second).astype(jnp.bfloat16)
    oth = jnp.where(core == 0, second, first).astype(jnp.bfloat16)
    own_first = jnp.concatenate([own, oth], axis=1)
    oth_first = jnp.concatenate([oth, own], axis=1)
    cols = blocks[0].shape[1]
    plan = [((own, blocks[0]), (oth, blocks[1]))]
    plan += [((oth_first if i in (1, 3, 5) else own_first, b),) for i, b in enumerate(blocks[2:])]
    for i, terms in enumerate(plan):
        out = sum(jnp.dot(a, w[...], preferred_element_type=jnp.float32) for a, w in terms)
        to = pl.multiple_of(info_ref[3 + i] * cols, DH)
        for chip in range(out_ref.shape[0]):
            out_ref[chip, :, pl.ds(to, cols)] = out[2 * chip : 2 * chip + 2].astype(jnp.bfloat16)


def body(
    queries,
    prefix_keys,
    prefix_values,
    suffix_keys,
    suffix_values,
    new_keys,
    new_values,
    suffix_lengths,
    counts,
    out_weight,
):
    bf16, f32, i32 = jnp.bfloat16, jnp.float32, jnp.int32
    samp = queries.shape[0]
    n_ctx = lax.axis_size("ctx")
    n_grp = lax.axis_size("group")
    chips = n_ctx // 2
    me = lax.axis_index("ctx")
    z = lax.axis_index("group")
    rows = samp * chips
    same_core = [[2 * d + k for d in range(chips)] for k in range(2)]

    def other_core(x):
        return lax.ppermute(x, "ctx", [(i, i ^ 1) for i in range(n_ctx)])

    def along_z(x):
        ring = [
            (g * n_ctx + c, (g + (1 if c % 2 == 0 else -1)) % n_grp * n_ctx + c)
            for g in range(n_grp)
            for c in range(n_ctx)
        ]
        return lax.ppermute(x, ("group", "ctx"), ring)

    def after(x, *earlier):
        return lax.optimization_barrier((x,) + earlier)[0]

    vmem = pl.BlockSpec(memory_space=pltpu.VMEM)
    smem = pl.BlockSpec(memory_space=pltpu.SMEM)
    hbm = pl.BlockSpec(memory_space=pl.ANY)

    with jax.named_scope("spread_queries"):
        spread = pl.pallas_call(
            spread_kernel,
            out_shape=jax.ShapeDtypeStruct((chips,) + queries.shape, bf16),
            in_specs=[vmem],
            out_specs=vmem,
            cost_estimate=pl.CostEstimate(flops=1, bytes_accessed=2**19, transcendentals=0),
        )(queries)
        q_own = lax.all_to_all(spread, "ctx", 0, 0, tiled=True, axis_index_groups=same_core)
        q_own = q_own.reshape(rows, QH * DH)

    with jax.named_scope("weights"):
        w_oth = other_core(out_weight)
        x1_own = along_z(out_weight)
        x1_oth = along_z(w_oth)

    table = []
    for g in range(n_grp):
        for c in range(n_ctx):
            way = 1 - 2 * (c % 2)
            home = samp * (c // 2)
            origin = [(g - way * by) % n_grp for by in (0, 1, -1, 2, -2, 3, -3, 4)]
            table.append([c % 2, home // ROWS, home % ROWS] + origin)
    info = lax.dynamic_index_in_dim(
        jnp.asarray(np.array(table, np.int32)), z * n_ctx + me, 0, keepdims=False
    )

    with jax.named_scope("suffix"):
        given = (queries, suffix_keys, suffix_values, new_keys, new_values)
        suffix = pl.pallas_call(
            suffix_kernel,
            out_shape=jax.ShapeDtypeStruct((KVH, GQ * samp, 3 * DH), f32),
            in_specs=[smem, smem] + [hbm] * 5,
            out_specs=vmem,
            scratch_shapes=[pltpu.VMEM(x.shape, x.dtype) for x in given]
            + [pltpu.SemaphoreType.DMA((5,))],
            compiler_params=pltpu.CompilerParams(vmem_limit_bytes=56 * 2**20),
            cost_estimate=pl.CostEstimate(flops=1, bytes_accessed=1, transcendentals=1),
        )(suffix_lengths, info, *given)

    with jax.named_scope("weights"):
        x1 = jnp.concatenate([x1_own, x1_oth], axis=0)

    with jax.named_scope("spread_queries"):
        q_oth = other_core(after(q_own, suffix, x1))

    with jax.named_scope("weights"):
        x2 = along_z(x1)
        e1 = other_core(x1)

    keeps, recvs = [], []
    with jax.named_scope("prefix"):
        prompts, positions, _ = prefix_keys.shape
        sent_rows = CHIP_HEADS * rows + MASS_ROWS
        tiles = 2 * rows // ROWS
        for n, heads in enumerate(SPLITS):
            at = sum(SPLITS[:n])
            q_block = pl.BlockSpec((rows, GQ * DH), lambda j, at=at: (0, at + j))
            kv_block = pl.BlockSpec(
                (prompts, positions, DH), lambda j, at=at: (0, 0, at + j)
            )
            suf_block = pl.BlockSpec(
                (1, GQ * samp, 3 * DH), lambda j, at=at: (at + j, 0, 0)
            )
            out_block = pl.BlockSpec((2, sent_rows, DH), lambda j: (j, 0, 0))
            keep, send = pl.pallas_call(
                prefix_kernel,
                out_shape=(
                    jax.ShapeDtypeStruct((2 * heads, sent_rows, DH), f32),
                    jax.ShapeDtypeStruct((2 * heads, sent_rows, DH), bf16),
                ),
                grid=(heads,),
                in_specs=[smem, smem, q_block, q_block, kv_block, kv_block, suf_block],
                out_specs=(out_block, out_block),
                scratch_shapes=[pltpu.VMEM((tiles, TILE, DH), f32)] * 3,
                compiler_params=pltpu.CompilerParams(vmem_limit_bytes=52 * 2**20),
                cost_estimate=pl.CostEstimate(
                    flops=2**31, bytes_accessed=2**23, transcendentals=2**22
                ),
            )(info, counts, q_own, q_oth, prefix_keys, prefix_values, suffix)
            keeps.append(keep)
            if n == 0:
                q_own, q_oth, x2, e1, send = lax.optimization_barrier(
                    (q_own, q_oth, x2, e1, send)
                )
            recvs.append(other_core(send))

    with jax.named_scope("weights"):
        x3 = along_z(x2)
        e2 = other_core(x2)

    with jax.named_scope("join_cores"):
        parts = pl.pallas_call(
            join_kernel,
            out_shape=jax.ShapeDtypeStruct((chips, sent_rows, DH), bf16),
            in_specs=[vmem] * (2 * len(SPLITS)),
            out_specs=vmem,
            compiler_params=pltpu.CompilerParams(vmem_limit_bytes=24 * 2**20),
        )(*keeps, *recvs)

    with jax.named_scope("weights"):
        parts, x3, e2 = lax.optimization_barrier((parts, x3, e2))
        e3 = other_core(x3)
        x4 = along_z(x3)
        blocks = (out_weight, w_oth, x1, e1, x2, e2, x3, e3, x4)

    with jax.named_scope("send_parts"):
        parts = lax.all_to_all(parts, "ctx", 0, 0, tiled=True, axis_index_groups=same_core)

    with jax.named_scope("project"):
        width = out_weight.shape[1]
        out = pl.pallas_call(
            project_kernel,
            out_shape=jax.ShapeDtypeStruct((chips, samp, n_grp * width), bf16),
            in_specs=[smem] + [vmem] * (1 + len(blocks)),
            out_specs=vmem,
            compiler_params=pltpu.CompilerParams(vmem_limit_bytes=20 * 2**20),
            cost_estimate=pl.CostEstimate(
                flops=2**28, bytes_accessed=2**23, transcendentals=2**12
            ),
        )(info, parts, *blocks)

    with jax.named_scope("send_rows"):
        out = lax.all_to_all(out, "ctx", 0, 0, tiled=True, axis_index_groups=same_core)
        return jnp.sum(out.astype(f32), axis=0).astype(bf16)


def solution(mesh):
    in_specs = (
        P(("group", "ctx"), None),
        P("group", "ctx", None),
        P("group", "ctx", None),
        P(("group", "ctx"), None, None),
        P(("group", "ctx"), None, None),
        P(("group", "ctx"), None),
        P(("group", "ctx"), None),
        P(("group", "ctx")),
        P("group"),
        P("ctx", "group"),
    )
    out_specs = P(("group", "ctx"), None)
    return jax.shard_map(body, mesh=mesh, in_specs=in_specs, out_specs=out_specs, check_vma=False)
```

```python
import math

import jax
import jax.numpy as jnp
import numpy as np
from jax import lax
from jax.experimental import pallas as pl
from jax.experimental.pallas import tpu as pltpu
from jax.sharding import PartitionSpec as P

QH = 64
KVH = 8
DH = 128
GQ = QH // KVH
CHIP_HEADS = 4
MASS_ROWS = 16
FLOOR = -1e30
SCALE = 1.0 / math.sqrt(DH)
ROWS = 16
TILE = ROWS * GQ
SPLITS = (5, 3)
CONTRACT = (((1,), (1,)), ((), ()))


def suffix_kernel(len_ref, info_ref, q_hbm, sk_hbm, sv_hbm, nk_hbm, nv_hbm, out_ref, q_ref, sk_ref, sv_ref, nk_ref, nv_ref, sems):
    pairs = (
        (q_hbm, q_ref),
        (nk_hbm, nk_ref),
        (nv_hbm, nv_ref),
        (sk_hbm, sk_ref),
        (sv_hbm, sv_ref),
    )
    copies = [pltpu.make_async_copy(a, b, sems.at[i]) for i, (a, b) in enumerate(pairs)]
    for c in copies:
        c.start()
    for c in copies:
        c.wait()
    samp, suf, _ = sk_ref.shape
    rows = GQ * samp
    row_samp = lax.broadcasted_iota(jnp.int32, (rows, suf), 0) % samp
    pos = lax.broadcasted_iota(jnp.int32, (rows, suf), 1)
    own = lax.broadcasted_iota(jnp.int32, (rows, DH), 0) % samp
    for h in range(KVH):
        cols = slice(h * DH, (h + 1) * DH)
        q = jnp.concatenate(
            [
                q_ref[:, (h * GQ + g) * DH : (h * GQ + g + 1) * DH].astype(jnp.float32)
                for g in range(GQ)
            ],
            axis=0,
        )
        q16 = q.astype(jnp.bfloat16)
        scores = []
        for j in range(samp):
            s = lax.dot_general(
                q16, sk_ref[j, :, cols], CONTRACT, preferred_element_type=jnp.float32
            )
            seen = (row_samp == j) & (pos < len_ref[j])
            scores.append(jnp.where(seen, s * SCALE, FLOOR))
        nk = jnp.zeros((rows, DH), jnp.float32)
        nv = jnp.zeros((rows, DH), jnp.float32)
        for j in range(samp):
            nk = jnp.where(own == j, nk_ref[j : j + 1, cols].astype(jnp.float32), nk)
            nv = jnp.where(own == j, nv_ref[j : j + 1, cols].astype(jnp.float32), nv)
        self_score = jnp.sum(q * nk, axis=1, keepdims=True) * SCALE
        peak = self_score
        for s in scores:
            peak = jnp.maximum(peak, jnp.max(s, axis=1, keepdims=True))
        self_term = jnp.exp(self_score - peak)
        total = self_term
        acc = self_term.astype(jnp.bfloat16).astype(jnp.float32) * nv
        for j in range(samp):
            terms = jnp.exp(scores[j] - peak)
            total = total + jnp.sum(terms, axis=1, keepdims=True)
            acc = acc + jnp.dot(
                terms.astype(jnp.bfloat16), sv_ref[j, :, cols], preferred_element_type=jnp.float32
            )
        out_ref[h, :, 0:DH] = acc
        out_ref[h, :, DH : 2 * DH] = jnp.broadcast_to(peak, (rows, DH))
        out_ref[h, :, 2 * DH : 3 * DH] = jnp.broadcast_to(total, (rows, DH))


def spread_kernel(q_ref, out_ref):
    for d in range(out_ref.shape[0]):
        out_ref[d] = q_ref[...]


def mass_block(mass, rows):
    high = mass.astype(jnp.bfloat16).astype(jnp.float32)
    mid = (mass - high).astype(jnp.bfloat16).astype(jnp.float32)
    row = lax.broadcasted_iota(jnp.int32, (rows, DH), 0)
    block = jnp.where(row == 0, high, jnp.where(row == 1, mid, mass - high - mid))
    return jnp.where(row < 3, block, 0.0)


def read_mass(ref):
    block = ref[:, ref.shape[1] - MASS_ROWS :, :].astype(jnp.float32)
    return block[:, 0] + block[:, 1] + block[:, 2]


def as_columns(x):
    parts = x.shape[0]
    return jnp.concatenate([x, jnp.zeros((DH - parts, DH), jnp.float32)], axis=0).T


def prefix_kernel(
    info_ref,
    counts_ref,
    q_own,
    q_oth,
    k_ref,
    v_ref,
    suf_ref,
    keep_ref,
    send_ref,
    acc_ref,
    peak_ref,
    total_ref,
):
    core = info_ref[0]
    positions = k_ref.shape[1]
    rows = q_own.shape[0]
    tiles = rows // ROWS
    visits = []
    for side, q_ref in enumerate((q_own, q_oth)):
        left = jnp.maximum(counts_ref[0] - 2 * (core if side == 0 else 1 - core), 0)
        count = 2 * (left // 4) + jnp.minimum(left % 4, 2)
        both = jnp.minimum(count // ROWS, tiles - 1)
        for i in range(tiles - 1):
            prompt = (i >= both).astype(jnp.int32)
            visits.append((side, q_ref, i + prompt, [prompt], count))
        visits.append((side, q_ref, both, [0, 1], count))

    def scores(visit):
        _, q_ref, tile, prompts, count = visit
        base = pl.multiple_of(tile * ROWS, ROWS)
        q = jnp.concatenate(
            [q_ref[pl.ds(base, ROWS), g * DH : (g + 1) * DH] for g in range(GQ)], axis=0
        )
        s = [
            lax.dot_general(q, k_ref[p], CONTRACT, preferred_element_type=jnp.float32)
            for p in prompts
        ]
        if len(s) == 1:
            return s[0]
        row = lax.broadcasted_iota(jnp.int32, (TILE, positions), 0) % ROWS + base
        return jnp.where(row < count, s[0], s[1])

    def weights(s, peak):
        terms = jnp.exp((s - peak) * SCALE)
        return terms.astype(jnp.bfloat16), peak, jnp.sum(terms, axis=1, keepdims=True)

    def values(visit, terms, peak, total):
        side, _, tile, prompts, count = visit
        acc = [jnp.dot(terms, v_ref[p], preferred_element_type=jnp.float32) for p in prompts]
        if len(acc) == 2:
            row = lax.broadcasted_iota(jnp.int32, (TILE, DH), 0) % ROWS + tile * ROWS
            acc = [jnp.where(row < count, acc[0], acc[1])]
        at = side * tiles + tile
        acc_ref[at] = acc[0]
        peak_ref[at] = jnp.broadcast_to(peak * SCALE, (TILE, DH))
        total_ref[at] = jnp.broadcast_to(total, (TILE, DH))

    def scored(visit):
        s = scores(visit)
        return s, jnp.max(s, axis=1, keepdims=True)

    ahead = scored(visits[0])
    behind = None
    for i, visit in enumerate(visits):
        now = ahead
        if i + 1 < len(visits):
            ahead = scored(visits[i + 1])
        if behind is not None:
            values(*behind)
        behind = (visit,) + weights(*now)
    values(*behind)

    home_tile = info_ref[1]
    home_row = info_ref[2]
    row = lax.broadcasted_iota(jnp.int32, (ROWS, DH), 0)
    for g in range(GQ):
        part = slice(g * ROWS, (g + 1) * ROWS)
        add = jnp.zeros((ROWS, DH), jnp.float32)
        add_peak = jnp.full((ROWS, DH), FLOOR, jnp.float32)
        add_total = jnp.zeros((ROWS, DH), jnp.float32)
        for j in range(2):
            here = row == home_row + j
            line = slice(2 * g + j, 2 * g + j + 1)
            add = jnp.where(here, suf_ref[0, line, 0:DH], add)
            add_peak = jnp.where(here, suf_ref[0, line, DH : 2 * DH], add_peak)
            add_total = jnp.where(here, suf_ref[0, line, 2 * DH : 3 * DH], add_total)
        peak = peak_ref[home_tile, part, :]
        top = jnp.maximum(peak, add_peak)
        a = jnp.exp(peak - top)
        b = jnp.exp(add_peak - top)
        acc_ref[home_tile, part, :] = acc_ref[home_tile, part, :] * a + add * b
        total_ref[home_tile, part, :] = total_ref[home_tile, part, :] * a + add_total * b
        peak_ref[home_tile, part, :] = top

    lane = lax.broadcasted_iota(jnp.int32, (ROWS, DH), 1)
    lines = [[None] * (CHIP_HEADS * tiles) for _ in range(4)]
    for side, out_ref in enumerate((keep_ref, send_ref)):
        for t in range(tiles):
            for g in range(GQ):
                chip, h = g // CHIP_HEADS, g % CHIP_HEADS
                part = slice(g * ROWS, (g + 1) * ROWS)
                total = total_ref[side * tiles + t, part, :]
                avg = acc_ref[side * tiles + t, part, :] / total
                at = h * rows + t * ROWS
                out_ref[chip, at : at + ROWS, :] = avg.astype(out_ref.dtype)
                lines[2 * side + chip][h * tiles + t] = peak_ref[
                    side * tiles + t, part, :
                ] + jnp.log(total)
    table = []
    for i in range(CHIP_HEADS * tiles):
        block = lines[0][i]
        for c in range(1, 4):
            block = jnp.where(lane == c, lines[c][i], block)
        table.append(block)
    table = jnp.concatenate(table, axis=0).T
    for side, out_ref in enumerate((keep_ref, send_ref)):
        for chip in range(2):
            c = 2 * side + chip
            block = mass_block(table[c : c + 1], MASS_ROWS)
            out_ref[chip, CHIP_HEADS * rows :, :] = block.astype(out_ref.dtype)


def join_kernel(*refs):
    out_ref = refs[-1]
    calls = len(SPLITS)
    at = 0
    for keep_ref, recv_ref in zip(refs[:calls], refs[calls : 2 * calls]):
        parts = keep_ref.shape[0]
        lines = keep_ref.shape[1] - MASS_ROWS
        masses = [read_mass(ref) for ref in (keep_ref, recv_ref)]
        top = jnp.maximum(*masses)
        shares = [jnp.exp(m - top) for m in masses]
        total = shares[0] + shares[1]
        weights = [as_columns(x / total) for x in shares]
        mass = top + jnp.log(total)
        for p in range(parts):
            a, b = [w[:, p : p + 1] for w in weights]
            acc = a * keep_ref[p, :lines, :] + b * recv_ref[p, :lines, :].astype(jnp.float32)
            out_ref[at + p, :lines, :] = acc.astype(jnp.bfloat16)
            block = mass_block(mass[p : p + 1], MASS_ROWS)
            out_ref[at + p, lines:, :] = block.astype(jnp.bfloat16)
        at += parts


def project_kernel(info_ref, parts_ref, *rest):
    blocks, out_ref = rest[:-1], rest[-1]
    core = info_ref[0]
    parts = parts_ref.shape[0]
    lines = parts_ref.shape[1] - MASS_ROWS
    rows = lines // CHIP_HEADS
    mass = read_mass(parts_ref)
    share = jnp.exp(mass - jnp.max(mass, axis=0, keepdims=True))
    flat = as_columns(share / jnp.sum(share, axis=0, keepdims=True))
    acc = jnp.zeros((lines, DH), jnp.float32)
    for p in range(parts):
        acc = acc + flat[:, p : p + 1] * parts_ref[p, :lines, :].astype(jnp.float32)
    heads = [acc[h * rows : (h + 1) * rows] for h in range(CHIP_HEADS)]
    half = CHIP_HEADS // 2
    first = jnp.concatenate(heads[:half], axis=1)
    second = jnp.concatenate(heads[half:], axis=1)
    own = jnp.where(core == 0, first, second).astype(jnp.bfloat16)
    oth = jnp.where(core == 0, second, first).astype(jnp.bfloat16)
    own_first = jnp.concatenate([own, oth], axis=1)
    oth_first = jnp.concatenate([oth, own], axis=1)
    cols = blocks[0].shape[1]
    plan = [((own, blocks[0]), (oth, blocks[1]))]
    plan += [((oth_first if i in (1, 3, 5) else own_first, b),) for i, b in enumerate(blocks[2:])]
    for i, terms in enumerate(plan):
        out = sum(jnp.dot(a, w[...], preferred_element_type=jnp.float32) for a, w in terms)
        to = pl.multiple_of(info_ref[3 + i] * cols, DH)
        for chip in range(out_ref.shape[0]):
            out_ref[chip, :, pl.ds(to, cols)] = out[2 * chip : 2 * chip + 2].astype(jnp.bfloat16)


def body(
    queries,
    prefix_keys,
    prefix_values,
    suffix_keys,
    suffix_values,
    new_keys,
    new_values,
    suffix_lengths,
    counts,
    out_weight,
):
    bf16, f32, i32 = jnp.bfloat16, jnp.float32, jnp.int32
    samp = queries.shape[0]
    n_ctx = lax.axis_size("ctx")
    n_grp = lax.axis_size("group")
    chips = n_ctx // 2
    me = lax.axis_index("ctx")
    z = lax.axis_index("group")
    rows = samp * chips
    same_core = [[2 * d + k for d in range(chips)] for k in range(2)]

    def other_core(x):
        return lax.ppermute(x, "ctx", [(i, i ^ 1) for i in range(n_ctx)])

    def along_z(x):
        ring = [
            (g * n_ctx + c, (g + (1 if c % 2 == 0 else -1)) % n_grp * n_ctx + c)
            for g in range(n_grp)
            for c in range(n_ctx)
        ]
        return lax.ppermute(x, ("group", "ctx"), ring)

    def after(x, *earlier):
        return lax.optimization_barrier((x,) + earlier)[0]

    vmem = pl.BlockSpec(memory_space=pltpu.VMEM)
    smem = pl.BlockSpec(memory_space=pltpu.SMEM)
    hbm = pl.BlockSpec(memory_space=pl.ANY)

    with jax.named_scope("spread_queries"):
        spread = pl.pallas_call(
            spread_kernel,
            out_shape=jax.ShapeDtypeStruct((chips,) + queries.shape, bf16),
            in_specs=[vmem],
            out_specs=vmem,
            cost_estimate=pl.CostEstimate(flops=1, bytes_accessed=2**19, transcendentals=0),
        )(queries)
        q_own = lax.all_to_all(spread, "ctx", 0, 0, tiled=True, axis_index_groups=same_core)
        q_own = q_own.reshape(rows, QH * DH)

    with jax.named_scope("weights"):
        w_oth = other_core(out_weight)
        x1_own = along_z(out_weight)
        x1_oth = along_z(w_oth)

    table = []
    for g in range(n_grp):
        for c in range(n_ctx):
            way = 1 - 2 * (c % 2)
            home = samp * (c // 2)
            origin = [(g - way * by) % n_grp for by in (0, 1, -1, 2, -2, 3, -3, 4)]
            table.append([c % 2, home // ROWS, home % ROWS] + origin)
    info = lax.dynamic_index_in_dim(
        jnp.asarray(np.array(table, np.int32)), z * n_ctx + me, 0, keepdims=False
    )

    with jax.named_scope("suffix"):
        given = (queries, suffix_keys, suffix_values, new_keys, new_values)
        suffix = pl.pallas_call(
            suffix_kernel,
            out_shape=jax.ShapeDtypeStruct((KVH, GQ * samp, 3 * DH), f32),
            in_specs=[smem, smem] + [hbm] * 5,
            out_specs=vmem,
            scratch_shapes=[pltpu.VMEM(x.shape, x.dtype) for x in given]
            + [pltpu.SemaphoreType.DMA((5,))],
            compiler_params=pltpu.CompilerParams(vmem_limit_bytes=56 * 2**20),
            cost_estimate=pl.CostEstimate(flops=1, bytes_accessed=1, transcendentals=1),
        )(suffix_lengths, info, *given)

    with jax.named_scope("weights"):
        x1 = jnp.concatenate([x1_own, x1_oth], axis=0)

    with jax.named_scope("spread_queries"):
        q_oth = other_core(after(q_own, suffix, x1))

    with jax.named_scope("weights"):
        x2 = along_z(x1)
        e1 = other_core(x1)

    keeps, recvs = [], []
    with jax.named_scope("prefix"):
        prompts, positions, _ = prefix_keys.shape
        sent_rows = CHIP_HEADS * rows + MASS_ROWS
        tiles = 2 * rows // ROWS
        for n, heads in enumerate(SPLITS):
            at = sum(SPLITS[:n])
            q_block = pl.BlockSpec((rows, GQ * DH), lambda j, at=at: (0, at + j))
            kv_block = pl.BlockSpec(
                (prompts, positions, DH), lambda j, at=at: (0, 0, at + j)
            )
            suf_block = pl.BlockSpec(
                (1, GQ * samp, 3 * DH), lambda j, at=at: (at + j, 0, 0)
            )
            out_block = pl.BlockSpec((2, sent_rows, DH), lambda j: (j, 0, 0))
            keep, send = pl.pallas_call(
                prefix_kernel,
                out_shape=(
                    jax.ShapeDtypeStruct((2 * heads, sent_rows, DH), f32),
                    jax.ShapeDtypeStruct((2 * heads, sent_rows, DH), bf16),
                ),
                grid=(heads,),
                in_specs=[smem, smem, q_block, q_block, kv_block, kv_block, suf_block],
                out_specs=(out_block, out_block),
                scratch_shapes=[pltpu.VMEM((tiles, TILE, DH), f32)] * 3,
                compiler_params=pltpu.CompilerParams(vmem_limit_bytes=48 * 2**20),
                cost_estimate=pl.CostEstimate(
                    flops=2**31, bytes_accessed=2**23, transcendentals=2**22
                ),
            )(info, counts, q_own, q_oth, prefix_keys, prefix_values, suffix)
            keeps.append(keep)
            if n == 0:
                q_own, q_oth, x2, e1, send = lax.optimization_barrier(
                    (q_own, q_oth, x2, e1, send)
                )
            recvs.append(other_core(send))

    with jax.named_scope("weights"):
        x3 = along_z(x2)
        e2 = other_core(x2)

    with jax.named_scope("join_cores"):
        parts = pl.pallas_call(
            join_kernel,
            out_shape=jax.ShapeDtypeStruct((chips, sent_rows, DH), bf16),
            in_specs=[vmem] * (2 * len(SPLITS)),
            out_specs=vmem,
            compiler_params=pltpu.CompilerParams(vmem_limit_bytes=24 * 2**20),
        )(*keeps, *recvs)

    with jax.named_scope("weights"):
        parts, e2 = lax.optimization_barrier((parts, e2))
        e3 = other_core(x3)
        x4 = along_z(x3)
        blocks = (out_weight, w_oth, x1, e1, x2, e2, x3, e3, x4)

    with jax.named_scope("send_parts"):
        parts = lax.all_to_all(parts, "ctx", 0, 0, tiled=True, axis_index_groups=same_core)

    with jax.named_scope("project"):
        width = out_weight.shape[1]
        out = pl.pallas_call(
            project_kernel,
            out_shape=jax.ShapeDtypeStruct((chips, samp, n_grp * width), bf16),
            in_specs=[smem] + [vmem] * (1 + len(blocks)),
            out_specs=vmem,
            compiler_params=pltpu.CompilerParams(vmem_limit_bytes=20 * 2**20),
            cost_estimate=pl.CostEstimate(
                flops=2**28, bytes_accessed=2**23, transcendentals=2**12
            ),
        )(info, parts, *blocks)

    with jax.named_scope("send_rows"):
        out = lax.all_to_all(out, "ctx", 0, 0, tiled=True, axis_index_groups=same_core)
        return jnp.sum(out.astype(f32), axis=0).astype(bf16)


def solution(mesh):
    in_specs = (
        P(("group", "ctx"), None),
        P("group", "ctx", None),
        P("group", "ctx", None),
        P(("group", "ctx"), None, None),
        P(("group", "ctx"), None, None),
        P(("group", "ctx"), None),
        P(("group", "ctx"), None),
        P(("group", "ctx")),
        P("group"),
        P("ctx", "group"),
    )
    out_specs = P(("group", "ctx"), None)
    return jax.shard_map(body, mesh=mesh, in_specs=in_specs, out_specs=out_specs, check_vma=False)
```
